256 devices in a mesh: tok: 32 (over x, y, core), col: 8 (over z).
Axes of the slice: x: 4, y: 4, z: 8, core: 2. Of those that a mesh axis runs over, the one named last changes fastest.
Arguments:
- features: bfloat16 [8192, 8192], P('tok', 'col'), may hold values from -6 to 6
- out_grad: bfloat16 [8192, 8192], P('tok', 'col'), may hold values from -6 to 6
- gate_pre: bfloat16 [8192, 14336], P('tok', 'col'), may hold values from -8 to 8
- up_pre: bfloat16 [8192, 14336], P('tok', 'col'), may hold values from -6 to 6
- hidden_grad: bfloat16 [8192, 14336], P('tok', 'col'), may hold values from -6 to 6
- block_hidden: int32 [3, 144], replicated, may hold values from 0 to 111, as said below
- block_feature: int32 [3, 144], replicated, may hold values from 0 to 63
- block_slot: int32 [3, 144], replicated, may hold values from 0 to 127, as said below
Outputs:
- block_grads: float32 [8, 128, 128, 128], P('col', 'tok')
The draws below stay inside these ranges and needn't reach their ends.
Inputs may be any that keep to these rules, and one draw needn't show every extreme that they name: `block_hidden`: within one matrix no (hidden, feature) pair repeats. Each shard of 14 consecutive hidden blocks holds at most 36 blocks of one matrix, and one shard holds exactly 36 blocks of each of the three matrices. `block_slot`: among the blocks of all three matrices whose hidden blocks lie in one shard the slots are distinct; slot // 4 is the owner; no owner holds more than 4 slots of one shard, and some owner holds exactly 4.
All inputs are finite; a program needn't handle non-finite values.
Results may differ from the reference program's by a relative error of at most 0.0029.
Values may be sent and summed in bfloat16 or wider, within the bound.
No kernel may reach another device: no remote copies, remote signals or barrier semaphores. Data moves between devices by JAX's collectives and lax.ppermute only.
A program may use at most 128 MiB of HBM per device.

```python
import math
import jax
import jax.numpy as jnp
from jax import lax

D = 8192
FFW = 14336
BS = 128
BLOCKS = 144
TOKENS = 8192
FB = 64
HB_DEV = 14
CAPC = 36
CAPO = 4
N_TOK = 32
N_COL = 8


def shuffle_cells(subkey):
    return jax.random.permutation(subkey, HB_DEV * FB).astype(jnp.int32)


def shuffle_owners(subkey):
    return jax.random.permutation(subkey, N_TOK).astype(jnp.int32)


def block_layout(key):
    heavy = jax.random.randint(jax.random.fold_in(key, 1), (), 0, N_COL)
    entry = jnp.arange(BLOCKS, dtype=jnp.int32)
    hid_all = []
    feat_all = []
    for matrix in range(3):
        mkey = jax.random.fold_in(key, 10 + matrix)
        offset = jnp.where(entry < CAPC, 0, 1 + (entry - CAPC) % (N_COL - 1))
        shard = (heavy + offset) % N_COL
        within = jnp.where(entry < CAPC, entry, (entry - CAPC) // (N_COL - 1))
        cells = jax.vmap(shuffle_cells)(jax.random.split(mkey, N_COL))
        position = cells[shard, within]
        order = jax.random.permutation(jax.random.fold_in(mkey, 7), BLOCKS)
        hid_all.append((shard * HB_DEV + position // FB)[order])
        feat_all.append((position % FB)[order])
    hidden = jnp.stack(hid_all).astype(jnp.int32)
    feature = jnp.stack(feat_all).astype(jnp.int32)
    group = hidden.reshape(-1) // HB_DEV
    onehot = (group[:, None] == jnp.arange(N_COL, dtype=jnp.int32)[None, :]).astype(jnp.int32)
    before = jnp.cumsum(onehot, axis=0) - onehot
    ranking = jnp.sum(before * onehot, axis=1)
    owners = jax.vmap(shuffle_owners)(jax.random.split(jax.random.fold_in(key, 2), N_COL))
    owner = owners[group, ranking % N_TOK]
    slots = (owner * CAPO + ranking // N_TOK).astype(jnp.int32)
    return (hidden, feature, slots.reshape(3, BLOCKS))


def draw_block_hidden(key, part):
    return block_layout(key)[0]


def draw_block_feature(key, part):
    return block_layout(key)[1]


def draw_block_slot(key, part):
    return block_layout(key)[2]


def levels(rng, shape, pieces, smallest, top_value):
    gain, own = 1.0, jax.random.fold_in(rng, 6)
    for axis_at, blocks in pieces:
        heights = jnp.exp(jax.random.uniform(jax.random.fold_in(own, axis_at), (blocks,), jnp.float32, smallest / len(pieces), top_value / len(pieces)))
        gain = gain * jnp.repeat(heights, shape[axis_at] // blocks).reshape([-1 if axis == axis_at else 1 for axis in range(len(shape))])
    return gain


def gaussian(rng, shape, spread, bound, cuts=(), kind=jnp.bfloat16):
    gain = levels(rng, shape, cuts, -0.22, 0.18) if cuts else 1.0
    drawn = jax.random.normal(rng, shape, jnp.float32) * spread * gain
    return jnp.minimum(jnp.maximum(drawn, -bound), bound).astype(kind)


def setup_inputs(seed: int = 0) -> dict:
    key_list = jax.random.split(jax.random.key(seed), 9)
    return {
        "features": gaussian(key_list[0], (TOKENS, D), 1.0, 6.0, ((0, 32), (1, 8))),
        "out_grad": gaussian(key_list[1], (TOKENS, D), 1.0, 6.0, ((0, 32), (1, 8))),
        "gate_pre": gaussian(key_list[2], (TOKENS, FFW), 1.5, 8.0, ((0, 32), (1, 8))),
        "up_pre": gaussian(key_list[3], (TOKENS, FFW), 1.0, 6.0, ((0, 32), (1, 8))),
        "hidden_grad": gaussian(key_list[4], (TOKENS, FFW), 1.0, 6.0, ((0, 32), (1, 8))),
        "block_hidden": draw_block_hidden(jax.random.fold_in(key_list[8], 71), 0),
        "block_feature": draw_block_feature(jax.random.fold_in(key_list[8], 71), 0),
        "block_slot": draw_block_slot(jax.random.fold_in(key_list[8], 71), 0),
    }


def hidden_side(matrix, gate_cols, up_cols, grad_cols):
    sig_val = jax.nn.sigmoid(gate_cols)
    act_val = gate_cols * sig_val
    if matrix == 0:
        result = grad_cols * up_cols * sig_val * (1.0 + gate_cols * (1.0 - sig_val))
    elif matrix == 1:
        result = grad_cols * act_val
    else:
        result = act_val * up_cols
    return result.astype(jnp.bfloat16)

def reference(features, out_grad, gate_pre, up_pre, hidden_grad, block_hidden, block_feature, block_slot):
    scaling = 1.0 / math.sqrt(TOKENS)
    slot_total = N_TOK * CAPO
    block_grads = jnp.zeros((N_COL * slot_total, BS, BS), jnp.float32)
    for matrix in range(3):

        def one_block(entry):
            hid_index = block_hidden[matrix, entry].astype(jnp.int32)
            feat_index = block_feature[matrix, entry].astype(jnp.int32)
            gate_cols = lax.dynamic_slice_in_dim(gate_pre, hid_index * BS, BS, 1).astype(jnp.float32)
            up_cols = lax.dynamic_slice_in_dim(up_pre, hid_index * BS, BS, 1).astype(jnp.float32)
            grad_cols = lax.dynamic_slice_in_dim(hidden_grad, hid_index * BS, BS, 1).astype(jnp.float32)
            hid_vals = hidden_side(matrix, gate_cols, up_cols, grad_cols)
            if matrix < 2:
                feat_vals = lax.dynamic_slice_in_dim(features, feat_index * BS, BS, 1)
                result = jnp.dot(feat_vals.T, hid_vals, preferred_element_type=jnp.float32)
            else:
                feat_vals = lax.dynamic_slice_in_dim(out_grad, feat_index * BS, BS, 1)
                result = jnp.dot(hid_vals.T, feat_vals, preferred_element_type=jnp.float32)
            return result * scaling
        tile_set = lax.map(one_block, jnp.arange(BLOCKS, dtype=jnp.int32))
        dest_index = (block_hidden[matrix] // HB_DEV).astype(jnp.int32) * slot_total + block_slot[matrix].astype(jnp.int32)
        block_grads = block_grads.at[dest_index].set(tile_set)
    return block_grads.reshape(N_COL, slot_total, BS, BS)
```

```python
import math

import jax
import jax.numpy as jnp
from jax import lax
from jax.experimental import pallas as pl
from jax.experimental.pallas import tpu as pltpu
from jax.sharding import PartitionSpec as P

BS = 128
NX, NY, NC = 4, 4, 2
CAPO = 4
F32, BF16 = jnp.float32, jnp.bfloat16
ANY = pl.BlockSpec(memory_space=pl.ANY)


def gate_kernel(gate_ref, up_ref, grad_ref, out_ref):
    gate = gate_ref[...].astype(F32)
    up = up_ref[...].astype(F32)
    grad = grad_ref[...].astype(F32)
    sig = jax.nn.sigmoid(gate)
    act = gate * sig
    out_ref[0, 0] = (grad * up * sig * (1.0 + gate * (1.0 - sig))).astype(BF16)
    out_ref[1, 0] = (grad * act).astype(BF16)
    out_ref[2, 0] = (act * up).astype(BF16)


def hidden_blocks(gate_pre, up_pre, hidden_grad):
    rows, width = gate_pre.shape
    blocks = width // BS
    spec = pl.BlockSpec((rows, BS), lambda i: (0, i))
    out = pl.pallas_call(
        gate_kernel,
        grid=(blocks,),
        in_specs=[spec] * 3,
        out_specs=pl.BlockSpec((3, 1, rows, BS), lambda i: (0, i, 0, 0)),
        out_shape=jax.ShapeDtypeStruct((3, blocks, rows, BS), BF16),
        cost_estimate=pl.CostEstimate(flops=0, bytes_accessed=6 * rows * width * 2, transcendentals=0),
        name="gate_blocks",
    )(gate_pre, up_pre, hidden_grad)
    return out.reshape(3 * blocks, rows, BS)


def tile_kernel(n_chunk, per, n_hid, scale, code_ref, *refs):
    chunks, (hid_ref, own_ref, send_ref, blk, sems) = refs[:n_chunk], refs[n_chunk:]
    copies = []
    for i, chunk in enumerate(chunks):
        for k in range(per):
            at = i * per + k
            copies.append(
                pltpu.make_async_copy(chunk.at[:, pl.ds(k * BS, BS)], blk.at[at], sems.at[at])
            )
    at = n_chunk * per
    copies.append(pltpu.make_async_copy(hid_ref, blk.at[pl.ds(at, n_hid)], sems.at[at]))
    for copy in copies:
        copy.start()
    for copy in copies:
        copy.wait()

    def tile(p):
        code = code_ref[p]
        found = jnp.maximum(code - 1, 0)
        left = blk[found // 256]
        right = blk[found % 256]
        out = lax.dot_general(left, right, (((0,), (0,)), ((), ())), preferred_element_type=F32)
        return out * jnp.where(code > 0, scale, 0.0)

    half = own_ref.shape[0]
    step = 4

    def own_body(i, carry):
        for k in range(step):
            own_ref[i * step + k] = tile(i * step + k)
        return carry

    def send_body(i, carry):
        for k in range(step):
            send_ref[i * step + k] = tile(half + i * step + k).astype(BF16)
        return carry

    lax.fori_loop(0, half // step, send_body, 0)
    lax.fori_loop(0, half // step, own_body, 0)


def make_tiles(codes, chunks, hid, scale):
    rows, width = chunks[0].shape
    per = width // BS
    n_chunk, n_hid = len(chunks), hid.shape[0]
    half = codes.shape[0] // 2
    blocks = n_chunk * per + n_hid

    def body(*refs):
        tile_kernel(n_chunk, per, n_hid, scale, *refs)

    return pl.pallas_call(
        body,
        in_specs=[pl.BlockSpec(memory_space=pltpu.SMEM)] + [ANY] * (n_chunk + 1),
        out_specs=[pl.BlockSpec(memory_space=pltpu.VMEM)] * 2,
        out_shape=[
            jax.ShapeDtypeStruct((half, BS, BS), F32),
            jax.ShapeDtypeStruct((half, BS, BS), BF16),
        ],
        scratch_shapes=[
            pltpu.VMEM((blocks, rows, BS), BF16),
            pltpu.SemaphoreType.DMA((n_chunk * per + 1,)),
        ],
        compiler_params=pltpu.CompilerParams(vmem_limit_bytes=40 * 2**20),
        name="tiles",
    )(codes, *chunks, hid)


def place():
    me = lax.axis_index("tok")
    return me // (NY * NC), (me // NC) % NY, me % NC


def shift_perm(axis, by):
    pairs = []
    for i in range(NX * NY * NC):
        x, y, c = i // (NY * NC), (i // NC) % NY, i % NC
        if axis == "x":
            x = (x + by) % NX
        elif axis == "y":
            y = (y + by) % NY
        else:
            c = (c + by) % NC
        pairs.append((i, (x * NY + y) * NC + c))
    return pairs


def shift(value, axis, by):
    return lax.ppermute(value, "tok", shift_perm(axis, by))


def slot_order():
    x, y, c = place()
    p = jnp.arange(NX * NY * NC * CAPO, dtype=jnp.int32)
    core, half, d1, d2, j = p // 64, (p // 32) % 2, (p // 8) % 4, (p // 2) % 4, p % 2
    to_x = (x + jnp.where(half == 0, d1, d2)) % NX
    to_y = (y + jnp.where(half == 0, d2, d1)) % NY
    to_c = (c + core) % NC
    return ((to_x * NY + to_y) * NC + to_c) * CAPO + half * 2 + j


def tile_codes(block_hidden, block_feature, block_slot, n_col, per, hid_per):
    col = lax.axis_index("col")
    matrix = jnp.arange(3, dtype=jnp.int32)[:, None]
    source = block_feature // per
    x_at = ((col - source) % n_col) * per + block_feature % per
    y_at = n_col * per + ((source - col) % n_col) * per + block_feature % per
    h_at = 2 * n_col * per + matrix * hid_per + block_hidden % hid_per
    left = jnp.where(matrix == 2, h_at, x_at)
    right = jnp.where(matrix == 2, y_at, h_at)
    here = block_hidden // hid_per == col
    value = jnp.where(here, 1 + left * 256 + right, 0).reshape(-1)
    hit = slot_order()[:, None] == block_slot.reshape(-1)[None, :]
    return jnp.sum(jnp.where(hit, value[None, :], 0), axis=1)


def first_stage(total, axis):
    cut = total.shape[1] // 2
    far = total[2].astype(BF16)
    up_far = shift(far[:cut], axis, 1)
    down_far = shift(far[cut:], axis, -1)
    near_up = jnp.concatenate([total[1, :cut] + up_far.astype(F32), total[1, cut:]]).astype(BF16)
    near_down = jnp.concatenate([total[3, :cut], total[3, cut:] + down_far.astype(F32)]).astype(BF16)
    from_down = shift(near_up, axis, 1)
    from_up = shift(near_down, axis, -1)
    return total[0] + from_down.astype(F32) + from_up.astype(F32)


def second_stage(total, axis):
    sent = total.astype(BF16)
    got = [shift(sent[k], axis, k) for k in (2, 1, 3)]
    out = total[0]
    for g in got:
        out = out + g.astype(F32)
    return out


def on_device(
    features, out_grad, gate_pre, up_pre, hidden_grad, block_hidden, block_feature, block_slot
):
    tok_rows = features.shape[0]
    n_col = lax.axis_size("col")
    scale = 1.0 / math.sqrt(tok_rows * lax.axis_size("tok"))
    forward = [(i, (i + 1) % n_col) for i in range(n_col)]
    back = [(i, (i - 1) % n_col) for i in range(n_col)]
    xs, ys = [features], [out_grad]
    for _ in range(n_col - 1):
        xs.append(lax.ppermute(xs[-1], "col", forward))
        ys.append(lax.ppermute(ys[-1], "col", back))
    hid = hidden_blocks(gate_pre, up_pre, hidden_grad)
    codes = tile_codes(
        block_hidden, block_feature, block_slot, n_col, features.shape[1] // BS, gate_pre.shape[1] // BS
    )
    own, send = make_tiles(codes, xs + ys, hid, scale)
    total = own + shift(send, "core", 1).astype(F32)
    total = total.reshape(2, 4, 4, 2, BS, BS)
    half_x = first_stage(total[0], "x")
    half_y = first_stage(total[1], "y")
    out_x = second_stage(half_x, "y")
    out_y = second_stage(half_y, "x")
    return jnp.concatenate([out_x, out_y])[None]


def solution(mesh):
    in_specs = (P("tok", "col"),) * 5 + (P(), P(), P())
    return jax.shard_map(
        on_device,
        mesh=mesh,
        in_specs=in_specs,
        out_specs=P("col", "tok", None, None),
        check_vma=False,
    )
```

```python
import math

import jax
import jax.numpy as jnp
from jax import lax
from jax.experimental import pallas as pl
from jax.experimental.pallas import tpu as pltpu
from jax.sharding import PartitionSpec as P

BS = 128
NX, NY, NC = 4, 4, 2
CAPO = 4
UNROLL = 4
F32, BF16 = jnp.float32, jnp.bfloat16
ANY = pl.BlockSpec(memory_space=pl.ANY)


def gate_kernel(gate_ref, up_ref, grad_ref, out_ref):
    gate = gate_ref[...].astype(F32)
    up = up_ref[...].astype(F32)
    grad = grad_ref[...].astype(F32)
    sig = jax.nn.sigmoid(gate)
    act = gate * sig
    out_ref[0, 0] = (grad * up * sig * (1.0 + gate * (1.0 - sig))).astype(BF16)
    out_ref[1, 0] = (grad * act).astype(BF16)
    out_ref[2, 0] = (act * up).astype(BF16)


def hidden_blocks(gate_pre, up_pre, hidden_grad):
    rows, width = gate_pre.shape
    blocks = width // BS
    spec = pl.BlockSpec((rows, BS), lambda i: (0, i))
    out = pl.pallas_call(
        gate_kernel,
        grid=(blocks,),
        in_specs=[spec] * 3,
        out_specs=pl.BlockSpec((3, 1, rows, BS), lambda i: (0, i, 0, 0)),
        out_shape=jax.ShapeDtypeStruct((3, blocks, rows, BS), BF16),
        cost_estimate=pl.CostEstimate(flops=0, bytes_accessed=6 * rows * width * 2, transcendentals=0),
        name="gate_blocks",
    )(gate_pre, up_pre, hidden_grad)
    return out.reshape(3 * blocks, rows, BS)


def tile_kernel(first, last, per, n_hid, scale, tab_ref, *refs):
    n_chunk = 4 * (last - first)
    chunks, hids = refs[:n_chunk], refs[n_chunk : n_chunk + 2]
    out_ref, blk, stage, zero, in_sems, out_sems, zero_sem = refs[-7:]
    rows = hids[0].shape[1]
    copies = []
    for i, chunk in enumerate(chunks):
        step, kind, core = i // 4, (i // 2) % 2, i % 2
        for k in range(per):
            at = (step * 2 + kind) * per + k
            copies.append(
                (chunk.at[:, pl.ds(k * BS, BS)], blk.at[at, pl.ds(core * rows, rows)])
            )
    n_feat = n_chunk // 2 * per
    for core in range(2):
        copies.append((hids[core], blk.at[pl.ds(n_feat, n_hid), pl.ds(core * rows, rows)]))
    copies = [pltpu.make_async_copy(a, b, in_sems.at[i]) for i, (a, b) in enumerate(copies)]
    for copy in copies:
        copy.start()

    places = out_ref.shape[0]
    begin, end = tab_ref[places + first], tab_ref[places + last]
    if first == 0:
        zero[...] = jnp.zeros_like(zero)
        empty = tab_ref[places + 8]

        def zero_start(i, carry):
            pltpu.make_async_copy(zero, out_ref.at[tab_ref[i] % 64], zero_sem).start()
            return carry

        def zero_wait(i, carry):
            pltpu.make_async_copy(zero, out_ref.at[tab_ref[i] % 64], zero_sem).wait()
            return carry

        lax.fori_loop(empty, places, zero_start, 0)
    for copy in copies:
        copy.wait()

    def tile(i):
        entry = tab_ref[jnp.minimum(i, end - 1)]
        hid = n_feat + (entry // 64) % 64
        feat = (entry // 4096) % 8
        down = (entry // (4096 * 64)) % 2
        step = (entry // (4096 * 8)) % 8
        feat = ((step - first) * 2 + down) * per + feat
        left = blk[jnp.where(down == 1, hid, feat)]
        right = blk[jnp.where(down == 1, feat, hid)]
        out = lax.dot_general(left, right, (((0,), (0,)), ((), ())), preferred_element_type=F32)
        return out * scale

    def put(n, k):
        i = begin + n * UNROLL + k
        at = (n % 2) * UNROLL + k
        entry = tab_ref[jnp.minimum(i, end - 1)]
        return pltpu.make_async_copy(stage.at[at], out_ref.at[entry % 64], out_sems.at[at])

    rounds = (end - begin + UNROLL - 1) // UNROLL

    def body(n, carry):
        @pl.when(n >= 2)
        def _():
            for k in range(UNROLL):
                put(n - 2, k).wait()

        made = [tile(begin + n * UNROLL + k) for k in range(UNROLL)]
        for k in range(UNROLL):
            stage[(n % 2) * UNROLL + k] = made[k]
        for k in range(UNROLL):

            @pl.when(begin + n * UNROLL + k < end)
            def _():
                put(n, k).start()

        return carry

    lax.fori_loop(0, rounds, body, 0)

    @pl.when(rounds >= 2)
    def _():
        for k in range(UNROLL):
            put(rounds - 2, k).wait()

    for k in range(UNROLL):

        @pl.when((rounds >= 1) & (begin + (rounds - 1) * UNROLL + k < end))
        def _():
            put(rounds - 1, k).wait()

    if first == 0:
        lax.fori_loop(empty, places, zero_wait, 0)


def make_tiles(first, last, table, chunks, hids, before, scale):
    rows, width = chunks[0].shape
    per = width // BS
    n_hid = hids[0].shape[0]
    places = NX * NY * CAPO
    blocks = len(chunks) // 2 * per + n_hid
    operands = (table, *chunks, *hids) + (() if before is None else (before,))

    def body(*refs):
        tile_kernel(first, last, per, n_hid, scale, *refs)

    return pl.pallas_call(
        body,
        in_specs=[pl.BlockSpec(memory_space=pltpu.SMEM)] + [ANY] * (len(operands) - 1),
        out_specs=ANY,
        out_shape=jax.ShapeDtypeStruct((places, BS, BS), F32),
        scratch_shapes=[
            pltpu.VMEM((blocks, 2 * rows, BS), BF16),
            pltpu.VMEM((2 * UNROLL, BS, BS), F32),
            pltpu.VMEM((BS, BS), F32),
            pltpu.SemaphoreType.DMA((len(chunks) * per + 2,)),
            pltpu.SemaphoreType.DMA((2 * UNROLL,)),
            pltpu.SemaphoreType.DMA,
        ],
        input_output_aliases={} if before is None else {len(operands) - 1: 0},
        cost_estimate=pl.CostEstimate(flops=2 * 8 * (last - first) * 512 * BS * BS, bytes_accessed=8 * 2**20, transcendentals=0),
        compiler_params=pltpu.CompilerParams(vmem_limit_bytes=60 * 2**20),
        name=f"tiles_{first}_{last}",
    )(*operands)


def place():
    me = lax.axis_index("tok")
    return me // (NY * NC), (me // NC) % NY, me % NC


def shift_perm(axis, by):
    pairs = []
    for i in range(NX * NY * NC):
        x, y, c = i // (NY * NC), (i // NC) % NY, i % NC
        if axis == "x":
            x = (x + by) % NX
        elif axis == "y":
            y = (y + by) % NY
        else:
            c = (c + by) % NC
        pairs.append((i, (x * NY + y) * NC + c))
    return pairs


def shift(value, axis, by):
    return lax.ppermute(value, "tok", shift_perm(axis, by))


def slot_order():
    x, y, c = place()
    p = jnp.arange(NX * NY * CAPO, dtype=jnp.int32)
    half, d1, d2, j = p // 32, (p // 8) % 4, (p // 2) % 4, p % 2
    to_x = (x + jnp.where(half == 0, d1, d2)) % NX
    to_y = (y + jnp.where(half == 0, d2, d1)) % NY
    return ((to_x * NY + to_y) * NC + c) * CAPO + half * 2 + j


def tile_table(block_hidden, block_feature, block_slot, n_col, per, hid_per):
    col = lax.axis_index("col")
    matrix = jnp.arange(3, dtype=jnp.int32)[:, None]
    source = block_feature // per
    down = (matrix == 2).astype(jnp.int32)
    step = jnp.where(down == 1, source - col, col - source) % n_col
    hid = matrix * hid_per + block_hidden % hid_per
    value = 1 + (((down * 8 + step) * 8 + block_feature % per) * 64 + hid)
    value = jnp.where(block_hidden // hid_per == col, value, 0).reshape(-1)
    hit = slot_order()[:, None] == block_slot.reshape(-1)[None, :]
    code = jnp.sum(jnp.where(hit, value[None, :], 0), axis=1)
    places = code.shape[0]
    p = jnp.arange(places, dtype=jnp.int32)
    entry = jnp.where(code > 0, (code - 1) * 64 + p, p)
    key = jnp.where(code > 0, (entry // (4096 * 8)) % 8, 8) * places + p
    rank = jnp.sum((key[None, :] < key[:, None]).astype(jnp.int32), axis=1)
    ordered = jnp.sum(jnp.where(rank[None, :] == p[:, None], entry[None, :], 0), axis=1)
    bounds = jnp.arange(16, dtype=jnp.int32) * places
    starts = jnp.sum((key[None, :] < bounds[:, None]).astype(jnp.int32), axis=1)
    return jnp.concatenate([ordered, starts])


def first_stage(total, axis):
    cut = total.shape[1] // 2
    far = total[2].astype(BF16)
    up_far = shift(far[:cut], axis, 1)
    down_far = shift(far[cut:], axis, -1)
    near_up = jnp.concatenate([total[1, :cut] + up_far.astype(F32), total[1, cut:]]).astype(BF16)
    near_down = jnp.concatenate([total[3, :cut], total[3, cut:] + down_far.astype(F32)]).astype(BF16)
    from_down = shift(near_up, axis, 1)
    from_up = shift(near_down, axis, -1)
    return total[0] + from_down.astype(F32) + from_up.astype(F32)


def second_stage(total, axis):
    sent = total.astype(BF16)
    got = [shift(sent[k], axis, k) for k in (2, 1, 3)]
    out = total[0]
    for g in got:
        out = out + g.astype(F32)
    return out


def on_device(
    features, out_grad, gate_pre, up_pre, hidden_grad, block_hidden, block_feature, block_slot
):
    tok_rows = features.shape[0]
    n_col = lax.axis_size("col")
    scale = 1.0 / math.sqrt(tok_rows * lax.axis_size("tok"))
    forward = [(i, (i + 1) % n_col) for i in range(n_col)]
    back = [(i, (i - 1) % n_col) for i in range(n_col)]
    table = tile_table(
        block_hidden, block_feature, block_slot, n_col, features.shape[1] // BS, gate_pre.shape[1] // BS
    )
    xs, ys = [features], [out_grad]
    pairs = []
    total = None
    for step in range(n_col):
        x, y = xs[-1], ys[-1]
        if step == 1:
            x, gates = lax.optimization_barrier((x, (gate_pre, up_pre, hidden_grad)))
            hid = hidden_blocks(*gates)
        if step == 2:
            x, y, hid, table = lax.optimization_barrier((x, y, hid, table))
            hids = (hid, shift(hid, "core", 1))
        if step == 4:
            x, y, hids = lax.optimization_barrier((x, y, hids))
        if step == 5:
            total = make_tiles(0, 4, table, sum(pairs[:4], []), hids, total, scale)
            x, y, total = lax.optimization_barrier((x, y, total))
        if step == n_col - 1:
            total = make_tiles(4, 7, table, sum(pairs[4:], []), hids, total, scale)
            x, y, total = lax.optimization_barrier((x, y, total))
        else:
            xs.append(lax.ppermute(x, "col", forward))
            ys.append(lax.ppermute(y, "col", back))
        pairs.append([x, shift(x, "core", 1), y, shift(y, "core", 1)])
    total = make_tiles(7, 8, table, pairs[7], hids, total, scale)
    total = total.reshape(2, 4, 4, 2, BS, BS)
    half_x = first_stage(total[0], "x")
    half_y = first_stage(total[1], "y")
    out_x = second_stage(half_x, "y")
    out_y = second_stage(half_y, "x")
    return jnp.concatenate([out_x, out_y])[None]


def solution(mesh):
    in_specs = (P("tok", "col"),) * 5 + (P(), P(), P())
    return jax.shard_map(
        on_device,
        mesh=mesh,
        in_specs=in_specs,
        out_specs=P("col", "tok", None, None),
        check_vma=False,
    )
```

```python
import math

import jax
import jax.numpy as jnp
from jax import lax
from jax.experimental import pallas as pl
from jax.experimental.pallas import tpu as pltpu
from jax.sharding import PartitionSpec as P

BS = 128
NX, NY, NC = 4, 4, 2
CAPO = 4
UNROLL = 4
PLACES = NX * NY * NC * CAPO
GROUPS = ((0, 16), (16, 48), (64, 16), (80, 48))
F32, BF16 = jnp.float32, jnp.bfloat16
ANY = pl.BlockSpec(memory_space=pl.ANY)


def gate_kernel(gate_ref, up_ref, grad_ref, out_ref):
    for k in range(out_ref.shape[1]):
        at = (slice(None), pl.ds(k * BS, BS))
        gate = gate_ref[at].astype(F32)
        up = up_ref[at].astype(F32)
        grad = grad_ref[at].astype(F32)
        sig = jax.nn.sigmoid(gate)
        act = gate * sig
        out_ref[0, k] = (grad * up * sig * (1.0 + gate * (1.0 - sig))).astype(BF16)
        out_ref[1, k] = (grad * act).astype(BF16)
        out_ref[2, k] = (act * up).astype(BF16)


def hidden_blocks(gate_pre, up_pre, hidden_grad):
    rows, width = gate_pre.shape
    blocks = width // BS
    each = blocks // 2
    spec = pl.BlockSpec((rows, each * BS), lambda i: (0, i))
    out = pl.pallas_call(
        gate_kernel,
        grid=(blocks // each,),
        in_specs=[spec] * 3,
        out_specs=pl.BlockSpec((3, each, rows, BS), lambda i: (0, i, 0, 0)),
        out_shape=jax.ShapeDtypeStruct((3, blocks, rows, BS), BF16),
        cost_estimate=pl.CostEstimate(flops=0, bytes_accessed=12 * rows * width * 2, transcendentals=0),
        compiler_params=pltpu.CompilerParams(vmem_limit_bytes=16 * 2**20),
        name="gate_blocks",
    )(gate_pre, up_pre, hidden_grad)
    return out.reshape(3 * blocks, rows, BS)


def tile_kernel(first, last, per, n_hid, scale, tab_ref, *refs):
    n_chunk = 2 * (last - first)
    chunks, hid_ref = refs[:n_chunk], refs[n_chunk]
    outs, (blk, stage, stage16, in_sems, out_sems) = refs[-9:-5], refs[-5:]
    copies = []
    for i, chunk in enumerate(chunks):
        for k in range(per):
            copies.append((chunk.at[:, pl.ds(k * BS, BS)], blk.at[i * per + k]))
    n_feat = n_chunk * per
    copies.append((hid_ref, blk.at[pl.ds(n_feat, n_hid)]))
    copies = [pltpu.make_async_copy(a, b, in_sems.at[i]) for i, (a, b) in enumerate(copies)]
    for copy in copies:
        copy.start()

    for copy in copies:
        copy.wait()

    for g, (base, size) in enumerate(GROUPS):
        begin, end = tab_ref[PLACES + g * 16 + first], tab_ref[PLACES + g * 16 + last]
        held = stage16 if outs[g].dtype == BF16 else stage

        def tile(i):
            entry = tab_ref[jnp.minimum(i, end - 1)] // PLACES
            hid = n_feat + entry % 64
            feat = (entry // 64) % 8
            step = (entry // 512) % 8
            down = entry // 4096
            feat = ((step - first) * 2 + down) * per + feat
            left = blk[jnp.where(down == 1, hid, feat)]
            right = blk[jnp.where(down == 1, feat, hid)]
            out = lax.dot_general(
                left, right, (((0,), (0,)), ((), ())), preferred_element_type=F32
            )
            return (out * scale).astype(held.dtype)

        def put(n, k):
            i = begin + n * UNROLL + k
            at = (n % 2) * UNROLL + k
            entry = tab_ref[jnp.minimum(i, end - 1)]
            return pltpu.make_async_copy(
                held.at[at], outs[g].at[entry % PLACES - base], out_sems.at[at]
            )

        rounds = (end - begin + UNROLL - 1) // UNROLL

        def body(n, carry):
            @pl.when(n >= 2)
            def _():
                for k in range(UNROLL):
                    put(n - 2, k).wait()

            made = [tile(begin + n * UNROLL + k) for k in range(UNROLL)]
            for k in range(UNROLL):
                held[(n % 2) * UNROLL + k] = made[k]
            for k in range(UNROLL):

                @pl.when(begin + n * UNROLL + k < end)
                def _():
                    put(n, k).start()

            return carry

        lax.fori_loop(0, rounds, body, 0)

        @pl.when(rounds >= 2)
        def _():
            for k in range(UNROLL):
                put(rounds - 2, k).wait()

        for k in range(UNROLL):

            @pl.when((rounds >= 1) & (begin + (rounds - 1) * UNROLL + k < end))
            def _():
                put(rounds - 1, k).wait()


def make_tiles(first, last, table, chunks, hid, before, scale):
    rows, width = chunks[0].shape
    per = width // BS
    n_hid = hid.shape[0]
    blocks = len(chunks) * per + n_hid
    operands = (table, *chunks, hid, *before)
    at = len(operands) - len(before)

    def body(*refs):
        tile_kernel(first, last, per, n_hid, scale, *refs)

    return pl.pallas_call(
        body,
        in_specs=[pl.BlockSpec(memory_space=pltpu.SMEM)] + [ANY] * (len(operands) - 1),
        out_specs=[ANY] * len(GROUPS),
        out_shape=[jax.ShapeDtypeStruct(b.shape, b.dtype) for b in before],
        scratch_shapes=[
            pltpu.VMEM((blocks, rows, BS), BF16),
            pltpu.VMEM((2 * UNROLL, BS, BS), F32),
            pltpu.VMEM((2 * UNROLL, BS, BS), BF16),
            pltpu.SemaphoreType.DMA((len(chunks) * per + 1,)),
            pltpu.SemaphoreType.DMA((2 * UNROLL,)),
        ],
        input_output_aliases={at + g: g for g in range(len(before))},
        cost_estimate=pl.CostEstimate(flops=0, bytes_accessed=10 * 2**20, transcendentals=0),
        compiler_params=pltpu.CompilerParams(vmem_limit_bytes=20 * 2**20),
        name=f"tiles_{first}_{last}",
    )(*operands)


def place():
    me = lax.axis_index("tok")
    return me // (NY * NC), (me // NC) % NY, me % NC


def shift(value, kind, by):
    pairs = []
    for i in range(NX * NY * NC):
        x, y, c = i // (NY * NC), (i // NC) % NY, i % NC
        if kind == "core":
            c = 1 - c
        elif kind == "first":
            x, y = ((x + by) % NX, y) if c == 0 else (x, (y + by) % NY)
        else:
            x, y = (x, y ^ by) if c == 0 else (x ^ by, y)
        pairs.append((i, (x * NY + y) * NC + c))
    return lax.ppermute(value, "tok", pairs)


def slot_order():
    x, y, c = place()
    p = jnp.arange(PLACES, dtype=jnp.int32)
    q = p % 64
    near = (q - 16) // 16
    d1 = jnp.where(q < 16, 2, jnp.where(near == 2, 3, near))
    d2 = (q // CAPO) % 4
    to_c = jnp.where(p < 64, 1 - c, c)
    to_x = jnp.where(to_c == 0, (x + d1) % NX, x ^ d2)
    to_y = jnp.where(to_c == 0, y ^ d2, (y + d1) % NY)
    return ((to_x * NY + to_y) * NC + to_c) * CAPO + p % CAPO


def tile_table(block_hidden, block_feature, block_slot, n_col, per, hid_per):
    col = lax.axis_index("col")
    matrix = jnp.arange(3, dtype=jnp.int32)[:, None]
    source = block_feature // per
    down = (matrix == 2).astype(jnp.int32)
    step = jnp.where(down == 1, source - col, col - source) % n_col
    hid = matrix * hid_per + block_hidden % hid_per
    value = 1 + (((down * 8 + step) * 8 + block_feature % per) * 64 + hid)
    value = jnp.where(block_hidden // hid_per == col, value, 0).reshape(-1)
    hit = slot_order()[:, None] == block_slot.reshape(-1)[None, :]
    code = jnp.sum(jnp.where(hit, value[None, :], 0), axis=1)
    p = jnp.arange(PLACES, dtype=jnp.int32)
    group = (p >= 16).astype(jnp.int32) + (p >= 64) + (p >= 80)
    entry = jnp.where(code > 0, (code - 1) * PLACES + p, p)
    came = jnp.where(code > 0, ((code - 1) // 512) % 8, 8)
    key = (group * 16 + came) * PLACES + p
    rank = jnp.sum((key[None, :] < key[:, None]).astype(jnp.int32), axis=1)
    ordered = jnp.sum(jnp.where(rank[None, :] == p[:, None], entry[None, :], 0), axis=1)
    bounds = jnp.arange(16 * len(GROUPS), dtype=jnp.int32) * PLACES
    starts = jnp.sum((key[None, :] < bounds[:, None]).astype(jnp.int32), axis=1)
    return jnp.concatenate([ordered, starts])


def reduce_tiles(send_far, send_rest, own_far, own_rest):
    got_far = shift(send_far, "core", 1)
    send_rest, got_far = lax.optimization_barrier((send_rest, got_far))
    got_rest = shift(send_rest, "core", 1)
    far = (own_far + got_far.astype(F32)).astype(BF16)
    from_down = shift(far[:8], "first", 1)
    from_up = shift(far[8:], "first", -1)
    here, up, down = (own_rest + got_rest.astype(F32)).reshape(3, 16, BS, BS)
    own_up = shift(up[8:].astype(BF16), "first", 1)
    own_down = shift(down[:8].astype(BF16), "first", -1)
    low = shift((up[:8] + from_down.astype(F32)).astype(BF16), "first", 1)
    high = shift((down[8:] + from_up.astype(F32)).astype(BF16), "first", -1)
    low = here[:8] + low.astype(F32) + own_down.astype(F32)
    high = here[8:] + high.astype(F32) + own_up.astype(F32)
    total = (*low.reshape(2, CAPO, BS, BS), *high.reshape(2, CAPO, BS, BS))
    out = total[0]
    for k in (2, 1, 3):
        out = out + shift(total[k].astype(BF16), "second", k).astype(F32)
    return out


def on_device(
    features, out_grad, gate_pre, up_pre, hidden_grad, block_hidden, block_feature, block_slot
):
    tok_rows = features.shape[0]
    n_col = lax.axis_size("col")
    scale = 1.0 / math.sqrt(tok_rows * lax.axis_size("tok"))
    forward = [(i, (i + 1) % n_col) for i in range(n_col)]
    back = [(i, (i - 1) % n_col) for i in range(n_col)]
    table = tile_table(
        block_hidden, block_feature, block_slot, n_col, features.shape[1] // BS, gate_pre.shape[1] // BS
    )
    tie = lax.optimization_barrier
    calls = {3: (0, 2), 4: (2, 3), 6: (3, 5), 7: (5, 7)}
    x, y = features, out_grad
    tiles = tuple(
        jnp.zeros((size, BS, BS), BF16 if g < 2 else F32) for g, (base, size) in enumerate(GROUPS)
    )
    chunks = []
    for step in range(n_col):
        if step == 1:
            x, tiles, gates = tie((x, tiles, (gate_pre, up_pre, hidden_grad)))
            hid = hidden_blocks(*gates)
        if step == 2:
            x, y, hid, table = tie((x, y, hid, table))
        if step in calls:
            first, last = calls[step]
            tiles = make_tiles(first, last, table, chunks[2 * first : 2 * last], hid, tiles, scale)
            x, y, tiles = tie((x, y, tiles))
        chunks += [x, y]
        if step < n_col - 1:
            x = lax.ppermute(x, "col", forward)
            y = lax.ppermute(y, "col", back)
    tiles = make_tiles(n_col - 1, n_col, table, chunks[-2:], hid, tiles, scale)
    return reduce_tiles(*tiles)[None]


def solution(mesh):
    in_specs = (P("tok", "col"),) * 5 + (P(), P(), P())
    return jax.shard_map(
        on_device,
        mesh=mesh,
        in_specs=in_specs,
        out_specs=P("col", "tok", None, None),
        check_vma=False,
    )
```

```python
import math

import jax
import jax.numpy as jnp
from jax import lax
from jax.experimental import pallas as pl
from jax.experimental.pallas import tpu as pltpu
from jax.sharding import PartitionSpec as P

BS = 128
NX, NY, NC = 4, 4, 2
CAPO = 4
UNROLL = 4
PLACES = NX * NY * NC * CAPO
GROUPS = ((0, 16), (16, 48), (64, 16), (80, 48))
F32, BF16 = jnp.float32, jnp.bfloat16
ANY = pl.BlockSpec(memory_space=pl.ANY)


def gate_kernel(gate_ref, up_ref, grad_ref, out_ref):
    for k in range(out_ref.shape[1]):
        at = (slice(None), pl.ds(k * BS, BS))
        gate = gate_ref[at].astype(F32)
        up = up_ref[at].astype(F32)
        grad = grad_ref[at].astype(F32)
        sig = jax.nn.sigmoid(gate)
        act = gate * sig
        out_ref[0, k] = (grad * up * sig * (1.0 + gate * (1.0 - sig))).astype(BF16)
        out_ref[1, k] = (grad * act).astype(BF16)
        out_ref[2, k] = (act * up).astype(BF16)


def hidden_blocks(gate_pre, up_pre, hidden_grad):
    rows, width = gate_pre.shape
    blocks = width // BS
    each = blocks // 2
    spec = pl.BlockSpec((rows, each * BS), lambda i: (0, i))
    out = pl.pallas_call(
        gate_kernel,
        grid=(blocks // each,),
        in_specs=[spec] * 3,
        out_specs=pl.BlockSpec((3, each, rows, BS), lambda i: (0, i, 0, 0)),
        out_shape=jax.ShapeDtypeStruct((3, blocks, rows, BS), BF16),
        cost_estimate=pl.CostEstimate(flops=0, bytes_accessed=12 * rows * width * 2, transcendentals=0),
        compiler_params=pltpu.CompilerParams(vmem_limit_bytes=16 * 2**20),
        name="gate_blocks",
    )(gate_pre, up_pre, hidden_grad)
    return out.reshape(3 * blocks, rows, BS)


def tile_kernel(segment, scale, tab_ref, chunk_ref, hid_ref, *refs):
    outs, (stage, stage16, sems) = refs[-7:-3], refs[-3:]
    begin, end = tab_ref[PLACES + segment], tab_ref[PLACES + segment + 1]
    rounds = (end - begin + UNROLL - 1) // UNROLL

    def tile(i):
        entry = tab_ref[jnp.minimum(i, end - 1)] // PLACES
        feat = chunk_ref[:, pl.ds(pl.multiple_of((entry // 64) % 8 * BS, BS), BS)]
        hid = hid_ref[entry % 64]
        left, right = (hid, feat) if segment % 2 else (feat, hid)
        out = lax.dot_general(left, right, (((0,), (0,)), ((), ())), preferred_element_type=F32)
        return out * scale

    def each_copy(n, k, act):
        i = begin + n * UNROLL + k
        at = (n % 2) * UNROLL + k
        p = tab_ref[jnp.minimum(i, end - 1)] % PLACES
        for g, (base, size) in enumerate(GROUPS):

            @pl.when((i < end) & (p >= base) & (p < base + size))
            def _():
                held = stage16 if outs[g].dtype == BF16 else stage
                act(pltpu.make_async_copy(held.at[at], outs[g].at[p - base], sems.at[at]))

    def start(copy):
        copy.start()

    def wait(copy):
        copy.wait()

    def body(n, carry):
        @pl.when(n >= 2)
        def _():
            for k in range(UNROLL):
                each_copy(n - 2, k, wait)

        made = [tile(begin + n * UNROLL + k) for k in range(UNROLL)]
        for k in range(UNROLL):
            stage[(n % 2) * UNROLL + k] = made[k]
            stage16[(n % 2) * UNROLL + k] = made[k].astype(BF16)
        for k in range(UNROLL):
            each_copy(n, k, start)
        return carry

    lax.fori_loop(0, rounds, body, 0)
    for back in (2, 1):

        @pl.when(rounds >= back)
        def _():
            for k in range(UNROLL):
                each_copy(rounds - back, k, wait)


def make_tiles(segment, table, chunk, hid, tiles, scale):
    def body(*refs):
        tile_kernel(segment, scale, *refs)

    return pl.pallas_call(
        body,
        in_specs=[
            pl.BlockSpec(memory_space=pltpu.SMEM),
            pl.BlockSpec(memory_space=pltpu.VMEM),
            pl.BlockSpec(memory_space=pltpu.VMEM),
            *[ANY] * len(tiles),
        ],
        out_specs=[ANY] * len(tiles),
        out_shape=[jax.ShapeDtypeStruct(t.shape, t.dtype) for t in tiles],
        scratch_shapes=[
            pltpu.VMEM((2 * UNROLL, BS, BS), F32),
            pltpu.VMEM((2 * UNROLL, BS, BS), BF16),
            pltpu.SemaphoreType.DMA((2 * UNROLL,)),
        ],
        input_output_aliases={3 + g: g for g in range(len(tiles))},
        cost_estimate=pl.CostEstimate(flops=0, bytes_accessed=4 * 2**20, transcendentals=0),
        compiler_params=pltpu.CompilerParams(vmem_limit_bytes=12 * 2**20),
        name=f"tiles_{segment}",
    )(table, chunk, hid, *tiles)


def place():
    me = lax.axis_index("tok")
    return me // (NY * NC), (me // NC) % NY, me % NC


def shift(value, kind, by):
    pairs = []
    for i in range(NX * NY * NC):
        x, y, c = i // (NY * NC), (i // NC) % NY, i % NC
        if kind == "core":
            c = 1 - c
        elif kind == "first":
            x, y = ((x + by) % NX, y) if c == 0 else (x, (y + by) % NY)
        else:
            x, y = (x, y ^ by) if c == 0 else (x ^ by, y)
        pairs.append((i, (x * NY + y) * NC + c))
    return lax.ppermute(value, "tok", pairs)


def slot_order():
    x, y, c = place()
    p = jnp.arange(PLACES, dtype=jnp.int32)
    q = p % 64
    near = (q - 16) // 16
    d1 = jnp.where(q < 16, 2, jnp.where(near == 2, 3, near))
    d2 = (q // CAPO) % 4
    to_c = jnp.where(p < 64, 1 - c, c)
    to_x = jnp.where(to_c == 0, (x + d1) % NX, x ^ d2)
    to_y = jnp.where(to_c == 0, y ^ d2, (y + d1) % NY)
    return ((to_x * NY + to_y) * NC + to_c) * CAPO + p % CAPO


def tile_table(block_hidden, block_feature, block_slot, n_col, per, hid_per):
    col = lax.axis_index("col")
    matrix = jnp.arange(3, dtype=jnp.int32)[:, None]
    down = (matrix == 2).astype(jnp.int32)
    ahead = jnp.where(place()[2] == 0, 1, -1)
    step = (ahead * (col - block_feature // per)) % n_col
    hid = matrix * hid_per + block_hidden % hid_per
    value = 1 + (((step * 2 + down) * 8 + block_feature % per) * 64 + hid)
    value = jnp.where(block_hidden // hid_per == col, value, 0).reshape(-1)
    hit = slot_order()[:, None] == block_slot.reshape(-1)[None, :]
    code = jnp.sum(jnp.where(hit, value[None, :], 0), axis=1)
    p = jnp.arange(PLACES, dtype=jnp.int32)
    entry = jnp.where(code > 0, (code - 1) * PLACES + p, p)
    key = jnp.where(code > 0, (code - 1) // 512, 2 * n_col) * PLACES + p
    rank = jnp.sum((key[None, :] < key[:, None]).astype(jnp.int32), axis=1)
    ordered = jnp.sum(jnp.where(rank[None, :] == p[:, None], entry[None, :], 0), axis=1)
    bounds = jnp.arange(24, dtype=jnp.int32) * PLACES
    starts = jnp.sum((key[None, :] < bounds[:, None]).astype(jnp.int32), axis=1)
    return jnp.concatenate([ordered, starts])


def reduce_tiles(send_far, send_rest, own_far, own_rest):
    got_far = shift(send_far, "core", 1)
    send_rest, got_far = lax.optimization_barrier((send_rest, got_far))
    got_rest = shift(send_rest, "core", 1)
    far = (own_far + got_far.astype(F32)).astype(BF16)
    from_down = shift(far[:8], "first", 1)
    from_up = shift(far[8:], "first", -1)
    here, up, down = (own_rest + got_rest.astype(F32)).reshape(3, 16, BS, BS)
    own_up = shift(up[8:].astype(BF16), "first", 1)
    own_down = shift(down[:8].astype(BF16), "first", -1)
    low = shift((up[:8] + from_down.astype(F32)).astype(BF16), "first", 1)
    high = shift((down[8:] + from_up.astype(F32)).astype(BF16), "first", -1)
    low = here[:8] + low.astype(F32) + own_down.astype(F32)
    high = here[8:] + high.astype(F32) + own_up.astype(F32)
    total = (*low.reshape(2, CAPO, BS, BS), *high.reshape(2, CAPO, BS, BS))
    out = total[0]
    for k in (2, 1, 3):
        out = out + shift(total[k].astype(BF16), "second", k).astype(F32)
    return out


def on_device(
    features, out_grad, gate_pre, up_pre, hidden_grad, block_hidden, block_feature, block_slot
):
    tok_rows = features.shape[0]
    n_col = lax.axis_size("col")
    scale = 1.0 / math.sqrt(tok_rows * lax.axis_size("tok"))
    ring = [
        (t * n_col + z, t * n_col + (z + (1 if t % NC == 0 else -1)) % n_col)
        for t in range(NX * NY * NC)
        for z in range(n_col)
    ]
    table = tile_table(
        block_hidden, block_feature, block_slot, n_col, features.shape[1] // BS, gate_pre.shape[1] // BS
    )
    hid = hidden_blocks(gate_pre, up_pre, hidden_grad)
    tiles = tuple(
        jnp.zeros((size, BS, BS), BF16 if g < 2 else F32) for g, (base, size) in enumerate(GROUPS)
    )
    tie = lax.optimization_barrier
    chunks = [features, out_grad]
    made = 0
    for segment in range(2, 2 * n_col):
        value = chunks[segment - 2]
        if segment == 4:
            value, table, hid, tiles = tie((value, table, hid, tiles))
        if segment > 4:
            tiles = make_tiles(made, table, chunks[made], hid, tiles, scale)
            made += 1
            value, tiles = tie((value, tiles))
        chunks.append(lax.ppermute(value, ("tok", "col"), ring))
    for segment in range(made, 2 * n_col):
        tiles = make_tiles(segment, table, chunks[segment], hid, tiles, scale)
    return reduce_tiles(*tiles)[None]


def solution(mesh):
    in_specs = (P("tok", "col"),) * 5 + (P(), P(), P())
    return jax.shard_map(
        on_device,
        mesh=mesh,
        in_specs=in_specs,
        out_specs=P("col", "tok", None, None),
        check_vma=False,
    )
```

```python
import math

import jax
import jax.numpy as jnp
from jax import lax
from jax.experimental import pallas as pl
from jax.experimental.pallas import tpu as pltpu
from jax.sharding import PartitionSpec as P

BS = 128
NX, NY, NC = 4, 4, 2
CAPO = 4
UNROLL = 4
PLACES = NX * NY * NC * CAPO
GROUPS = ((0, 32), (32, 32), (64, 32), (96, 32))
F32, BF16 = jnp.float32, jnp.bfloat16
ANY = pl.BlockSpec(memory_space=pl.ANY)


def gate_kernel(gate_ref, up_ref, grad_ref, out_ref):
    for k in range(out_ref.shape[1]):
        at = (slice(None), pl.ds(k * BS, BS))
        gate = gate_ref[at].astype(F32)
        up = up_ref[at].astype(F32)
        grad = grad_ref[at].astype(F32)
        sig = jax.nn.sigmoid(gate)
        act = gate * sig
        out_ref[0, k] = (grad * up * sig * (1.0 + gate * (1.0 - sig))).astype(BF16)
        out_ref[1, k] = (grad * act).astype(BF16)
        out_ref[2, k] = (act * up).astype(BF16)


def hidden_blocks(gate_pre, up_pre, hidden_grad):
    rows, width = gate_pre.shape
    blocks = width // BS
    each = blocks // 2
    spec = pl.BlockSpec((rows, each * BS), lambda i: (0, i))
    out = pl.pallas_call(
        gate_kernel,
        grid=(blocks // each,),
        in_specs=[spec] * 3,
        out_specs=pl.BlockSpec((3, each, rows, BS), lambda i: (0, i, 0, 0)),
        out_shape=jax.ShapeDtypeStruct((3, blocks, rows, BS), BF16),
        cost_estimate=pl.CostEstimate(flops=0, bytes_accessed=12 * rows * width * 2, transcendentals=0),
        compiler_params=pltpu.CompilerParams(vmem_limit_bytes=16 * 2**20),
        name="gate_blocks",
    )(gate_pre, up_pre, hidden_grad)
    return out.reshape(3 * blocks, rows, BS)


def tile_kernel(segment, scale, tab_ref, chunk_ref, hid_ref, *refs):
    outs, (stage, stage16, sems) = refs[-7:-3], refs[-3:]
    begin, end = tab_ref[PLACES + segment], tab_ref[PLACES + segment + 1]
    rounds = (end - begin + UNROLL - 1) // UNROLL

    def tile(i):
        entry = tab_ref[jnp.minimum(i, end - 1)] // PLACES
        feat = chunk_ref[:, pl.ds(pl.multiple_of((entry // 64) % 8 * BS, BS), BS)]
        hid = hid_ref[entry % 64]
        left, right = (hid, feat) if segment % 2 else (feat, hid)
        out = lax.dot_general(left, right, (((0,), (0,)), ((), ())), preferred_element_type=F32)
        return out * scale

    def each_copy(n, k, act):
        i = begin + n * UNROLL + k
        at = (n % 2) * UNROLL + k
        p = tab_ref[jnp.minimum(i, end - 1)] % PLACES
        for g, (base, size) in enumerate(GROUPS):

            @pl.when((i < end) & (p >= base) & (p < base + size))
            def _():
                held = stage16 if outs[g].dtype == BF16 else stage
                act(pltpu.make_async_copy(held.at[at], outs[g].at[p - base], sems.at[at]))

    def start(copy):
        copy.start()

    def wait(copy):
        copy.wait()

    def body(n, carry):
        @pl.when(n >= 2)
        def _():
            for k in range(UNROLL):
                each_copy(n - 2, k, wait)

        made = [tile(begin + n * UNROLL + k) for k in range(UNROLL)]
        for k in range(UNROLL):
            stage[(n % 2) * UNROLL + k] = made[k]
            stage16[(n % 2) * UNROLL + k] = made[k].astype(BF16)
        for k in range(UNROLL):
            each_copy(n, k, start)
        return carry

    lax.fori_loop(0, rounds, body, 0)
    for back in (2, 1):

        @pl.when(rounds >= back)
        def _():
            for k in range(UNROLL):
                each_copy(rounds - back, k, wait)


def make_tiles(segment, table, chunk, hid, tiles, scale):
    def body(*refs):
        tile_kernel(segment, scale, *refs)

    return pl.pallas_call(
        body,
        in_specs=[
            pl.BlockSpec(memory_space=pltpu.SMEM),
            pl.BlockSpec(memory_space=pltpu.VMEM),
            pl.BlockSpec(memory_space=pltpu.VMEM),
            *[ANY] * len(tiles),
        ],
        out_specs=[ANY] * len(tiles),
        out_shape=[jax.ShapeDtypeStruct(t.shape, t.dtype) for t in tiles],
        scratch_shapes=[
            pltpu.VMEM((2 * UNROLL, BS, BS), F32),
            pltpu.VMEM((2 * UNROLL, BS, BS), BF16),
            pltpu.SemaphoreType.DMA((2 * UNROLL,)),
        ],
        input_output_aliases={3 + g: g for g in range(len(tiles))},
        cost_estimate=pl.CostEstimate(flops=0, bytes_accessed=4 * 2**20, transcendentals=0),
        compiler_params=pltpu.CompilerParams(vmem_limit_bytes=12 * 2**20),
        name=f"tiles_{segment}",
    )(table, chunk, hid, *tiles)


def place():
    me = lax.axis_index("tok")
    return me // (NY * NC), (me // NC) % NY, me % NC


def shift(value, kind, by):
    pairs = []
    for i in range(NX * NY * NC):
        x, y, c = i // (NY * NC), (i // NC) % NY, i % NC
        if kind == "core":
            c = 1 - c
        elif kind == "first":
            x, y = ((x + by) % NX, y) if c == 0 else (x, (y + by) % NY)
        else:
            x, y = (x, y ^ by) if c == 0 else (x ^ by, y)
        pairs.append((i, (x * NY + y) * NC + c))
    return lax.ppermute(value, "tok", pairs)


def slot_order():
    x, y, c = place()
    p = jnp.arange(PLACES, dtype=jnp.int32)
    b = (p // 8) % 8
    d1 = jnp.where((b == 1) | (b == 4), 1, jnp.where((b == 0) | (b == 2), 2, jnp.where(b < 6, 3, 0)))
    upper = (b == 1) | (b == 2) | (b == 5) | (b == 7)
    d2 = (p // CAPO) % 2 + 2 * upper.astype(jnp.int32)
    to_c = jnp.where(p < 64, 1 - c, c)
    to_x = jnp.where(to_c == 0, (x + d1) % NX, x ^ d2)
    to_y = jnp.where(to_c == 0, y ^ d2, (y + d1) % NY)
    return ((to_x * NY + to_y) * NC + to_c) * CAPO + p % CAPO


def tile_table(block_hidden, block_feature, block_slot, n_col, per, hid_per):
    col = lax.axis_index("col")
    matrix = jnp.arange(3, dtype=jnp.int32)[:, None]
    down = (matrix == 2).astype(jnp.int32)
    ahead = jnp.where(place()[2] == 0, 1, -1)
    step = (ahead * (col - block_feature // per)) % n_col
    hid = matrix * hid_per + block_hidden % hid_per
    value = 1 + (((step * 2 + down) * 8 + block_feature % per) * 64 + hid)
    value = jnp.where(block_hidden // hid_per == col, value, 0).reshape(-1)
    hit = slot_order()[:, None] == block_slot.reshape(-1)[None, :]
    code = jnp.sum(jnp.where(hit, value[None, :], 0), axis=1)
    p = jnp.arange(PLACES, dtype=jnp.int32)
    entry = jnp.where(code > 0, (code - 1) * PLACES + p, p)
    key = jnp.where(code > 0, (code - 1) // 512, 2 * n_col) * PLACES + p
    rank = jnp.sum((key[None, :] < key[:, None]).astype(jnp.int32), axis=1)
    ordered = jnp.sum(jnp.where(rank[None, :] == p[:, None], entry[None, :], 0), axis=1)
    bounds = jnp.arange(24, dtype=jnp.int32) * PLACES
    starts = jnp.sum((key[None, :] < bounds[:, None]).astype(jnp.int32), axis=1)
    return jnp.concatenate([ordered, starts])


def reduce_tiles(send_now, send_rest, own_now, own_rest):
    tie = lax.optimization_barrier
    got_now = shift(send_now, "core", 1)
    send_rest, got_now = tie((send_rest, got_now))
    got_rest = shift(send_rest, "core", 1)
    now = (own_now + got_now.astype(F32)).astype(BF16)
    up, down = tie((now[:16], now[16:]))
    up = shift(up, "first", 1)
    down = shift(down, "first", -1)
    rest = own_rest + got_rest.astype(F32)
    rest, up, down = tie((rest, up, down))
    low, high = tie(
        (
            (rest[:8] + up[:8].astype(F32)).astype(BF16),
            (rest[8:16] + down[:8].astype(F32)).astype(BF16),
        )
    )
    low = shift(low, "first", 1)
    high = shift(high, "first", -1)
    low, high = tie((low, high))
    low = rest[16:24] + low.astype(F32) + down[8:].astype(F32)
    high = rest[24:] + high.astype(F32) + up[8:].astype(F32)
    total = (*low.reshape(2, CAPO, BS, BS), *high.reshape(2, CAPO, BS, BS))
    out, *sent = tie((total[0], *(total[k].astype(BF16) for k in (2, 1, 3))))
    got = tie(tuple(shift(value, "second", k) for value, k in zip(sent, (2, 1, 3))))
    for value in got:
        out = out + value.astype(F32)
    return out


def on_device(
    features, out_grad, gate_pre, up_pre, hidden_grad, block_hidden, block_feature, block_slot
):
    tok_rows = features.shape[0]
    n_col = lax.axis_size("col")
    scale = 1.0 / math.sqrt(tok_rows * lax.axis_size("tok"))
    ring = [
        (t * n_col + z, t * n_col + (z + (1 if t % NC == 0 else -1)) % n_col)
        for t in range(NX * NY * NC)
        for z in range(n_col)
    ]
    table = tile_table(
        block_hidden, block_feature, block_slot, n_col, features.shape[1] // BS, gate_pre.shape[1] // BS
    )
    hid = hidden_blocks(gate_pre, up_pre, hidden_grad)
    tiles = tuple(
        jnp.zeros((size, BS, BS), BF16 if g < 2 else F32) for g, (base, size) in enumerate(GROUPS)
    )
    tie = lax.optimization_barrier
    chunks = [features, out_grad]
    made = 0
    for segment in range(2, 2 * n_col):
        value = chunks[segment - 2]
        if segment == 4:
            value, table, hid, tiles = tie((value, table, hid, tiles))
        if segment > 4:
            tiles = make_tiles(made, table, chunks[made], hid, tiles, scale)
            made += 1
            value, tiles = tie((value, tiles))
        chunks.append(lax.ppermute(value, ("tok", "col"), ring))
    for segment in range(made, 2 * n_col):
        tiles = make_tiles(segment, table, chunks[segment], hid, tiles, scale)
    return reduce_tiles(*tiles)[None]


def solution(mesh):
    in_specs = (P("tok", "col"),) * 5 + (P(), P(), P())
    return jax.shard_map(
        on_device,
        mesh=mesh,
        in_specs=in_specs,
        out_specs=P("col", "tok", None, None),
        check_vma=False,
    )
```

```python
import math

import jax
import jax.numpy as jnp
from jax import lax
from jax.experimental import pallas as pl
from jax.experimental.pallas import tpu as pltpu
from jax.sharding import PartitionSpec as P

BS = 128
NX, NY, NC = 4, 4, 2
CAPO = 4
UNROLL = 4
PLACES = NX * NY * NC * CAPO
GROUPS = ((0, 16), (16, 48), (64, 16), (80, 48))
F32, BF16 = jnp.float32, jnp.bfloat16
ANY = pl.BlockSpec(memory_space=pl.ANY)


def gate_kernel(gate_ref, up_ref, grad_ref, out_ref):
    for k in range(out_ref.shape[1]):
        at = (slice(None), pl.ds(k * BS, BS))
        gate = gate_ref[at].astype(F32)
        up = up_ref[at].astype(F32)
        grad = grad_ref[at].astype(F32)
        sig = jax.nn.sigmoid(gate)
        act = gate * sig
        out_ref[0, k] = (grad * up * sig * (1.0 + gate * (1.0 - sig))).astype(BF16)
        out_ref[1, k] = (grad * act).astype(BF16)
        out_ref[2, k] = (act * up).astype(BF16)


def hidden_blocks(gate_pre, up_pre, hidden_grad):
    rows, width = gate_pre.shape
    blocks = width // BS
    each = blocks // 2
    spec = pl.BlockSpec((rows, each * BS), lambda i: (0, i))
    out = pl.pallas_call(
        gate_kernel,
        grid=(blocks // each,),
        in_specs=[spec] * 3,
        out_specs=pl.BlockSpec((3, each, rows, BS), lambda i: (0, i, 0, 0)),
        out_shape=jax.ShapeDtypeStruct((3, blocks, rows, BS), BF16),
        cost_estimate=pl.CostEstimate(flops=0, bytes_accessed=12 * rows * width * 2, transcendentals=0),
        compiler_params=pltpu.CompilerParams(vmem_limit_bytes=16 * 2**20),
        name="gate_blocks",
    )(gate_pre, up_pre, hidden_grad)
    return out.reshape(3 * blocks, rows, BS)


def tile_kernel(segment, scale, tab_ref, chunk_ref, hid_ref, *refs):
    outs, (stage, stage16, sems) = refs[-7:-3], refs[-3:]
    begin, end = tab_ref[PLACES + segment], tab_ref[PLACES + segment + 1]
    rounds = (end - begin + UNROLL - 1) // UNROLL

    def tile(i):
        entry = tab_ref[jnp.minimum(i, end - 1)] // PLACES
        feat = chunk_ref[:, pl.ds(pl.multiple_of((entry // 64) % 8 * BS, BS), BS)]
        hid = hid_ref[entry % 64]
        left, right = (hid, feat) if segment % 2 else (feat, hid)
        out = lax.dot_general(left, right, (((0,), (0,)), ((), ())), preferred_element_type=F32)
        return out * scale

    def each_copy(n, k, act):
        i = begin + n * UNROLL + k
        at = (n % 2) * UNROLL + k
        p = tab_ref[jnp.minimum(i, end - 1)] % PLACES
        for g, (base, size) in enumerate(GROUPS):

            @pl.when((i < end) & (p >= base) & (p < base + size))
            def _():
                held = stage16 if outs[g].dtype == BF16 else stage
                act(pltpu.make_async_copy(held.at[at], outs[g].at[p - base], sems.at[at]))

    def start(copy):
        copy.start()

    def wait(copy):
        copy.wait()

    def body(n, carry):
        @pl.when(n >= 2)
        def _():
            for k in range(UNROLL):
                each_copy(n - 2, k, wait)

        made = [tile(begin + n * UNROLL + k) for k in range(UNROLL)]
        for k in range(UNROLL):
            stage[(n % 2) * UNROLL + k] = made[k]
            stage16[(n % 2) * UNROLL + k] = made[k].astype(BF16)
        for k in range(UNROLL):
            each_copy(n, k, start)
        return carry

    lax.fori_loop(0, rounds, body, 0)
    for back in (2, 1):

        @pl.when(rounds >= back)
        def _():
            for k in range(UNROLL):
                each_copy(rounds - back, k, wait)


def make_tiles(segment, table, chunk, hid, tiles, scale):
    def body(*refs):
        tile_kernel(segment, scale, *refs)

    return pl.pallas_call(
        body,
        in_specs=[
            pl.BlockSpec(memory_space=pltpu.SMEM),
            pl.BlockSpec(memory_space=pltpu.VMEM),
            pl.BlockSpec(memory_space=pltpu.VMEM),
            *[ANY] * len(tiles),
        ],
        out_specs=[ANY] * len(tiles),
        out_shape=[jax.ShapeDtypeStruct(t.shape, t.dtype) for t in tiles],
        scratch_shapes=[
            pltpu.VMEM((2 * UNROLL, BS, BS), F32),
            pltpu.VMEM((2 * UNROLL, BS, BS), BF16),
            pltpu.SemaphoreType.DMA((2 * UNROLL,)),
        ],
        input_output_aliases={3 + g: g for g in range(len(tiles))},
        cost_estimate=pl.CostEstimate(flops=0, bytes_accessed=4 * 2**20, transcendentals=0),
        compiler_params=pltpu.CompilerParams(vmem_limit_bytes=12 * 2**20),
        name=f"tiles_{segment}",
    )(table, chunk, hid, *tiles)


def place():
    me = lax.axis_index("tok")
    return me // (NY * NC), (me // NC) % NY, me % NC


def shift(value, kind, by):
    pairs = []
    for i in range(NX * NY * NC):
        x, y, c = i // (NY * NC), (i // NC) % NY, i % NC
        if kind == "core":
            c = 1 - c
        elif kind == "first":
            x, y = ((x + by) % NX, y) if c == 0 else (x, (y + by) % NY)
        else:
            x, y = (x, y ^ by) if c == 0 else (x ^ by, y)
        pairs.append((i, (x * NY + y) * NC + c))
    return lax.ppermute(value, "tok", pairs)


def slot_order():
    x, y, c = place()
    p = jnp.arange(PLACES, dtype=jnp.int32)
    b = (p // 8) % 8
    d1 = jnp.where(b < 2, 2, jnp.where(b < 4, 1, jnp.where(b < 6, 3, 0)))
    upper = (b == 1) | (b == 3) | (b == 4) | (b == 7)
    d2 = (p // CAPO) % 2 + 2 * upper.astype(jnp.int32)
    to_c = jnp.where(p < 64, 1 - c, c)
    to_x = jnp.where(to_c == 0, (x + d1) % NX, x ^ d2)
    to_y = jnp.where(to_c == 0, y ^ d2, (y + d1) % NY)
    return ((to_x * NY + to_y) * NC + to_c) * CAPO + p % CAPO


def tile_table(block_hidden, block_feature, block_slot, n_col, per, hid_per):
    col = lax.axis_index("col")
    matrix = jnp.arange(3, dtype=jnp.int32)[:, None]
    down = (matrix == 2).astype(jnp.int32)
    ahead = jnp.where(place()[2] == 0, 1, -1)
    step = (ahead * (col - block_feature // per)) % n_col
    hid = matrix * hid_per + block_hidden % hid_per
    value = 1 + (((step * 2 + down) * 8 + block_feature % per) * 64 + hid)
    value = jnp.where(block_hidden // hid_per == col, value, 0).reshape(-1)
    hit = slot_order()[:, None] == block_slot.reshape(-1)[None, :]
    code = jnp.sum(jnp.where(hit, value[None, :], 0), axis=1)
    p = jnp.arange(PLACES, dtype=jnp.int32)
    entry = jnp.where(code > 0, (code - 1) * PLACES + p, p)
    key = jnp.where(code > 0, (code - 1) // 512, 2 * n_col) * PLACES + p
    rank = jnp.sum((key[None, :] < key[:, None]).astype(jnp.int32), axis=1)
    ordered = jnp.sum(jnp.where(rank[None, :] == p[:, None], entry[None, :], 0), axis=1)
    bounds = jnp.arange(24, dtype=jnp.int32) * PLACES
    starts = jnp.sum((key[None, :] < bounds[:, None]).astype(jnp.int32), axis=1)
    return jnp.concatenate([ordered, starts])


def reduce_tiles(send_now, send_rest, own_now, own_rest):
    tie = lax.optimization_barrier
    got_now = shift(send_now, "core", 1)
    send_rest, got_now = tie((send_rest, got_now))
    got_rest = shift(send_rest, "core", 1)
    now = (own_now + got_now.astype(F32)).astype(BF16)
    up, down = tie((now[:8], now[8:]))
    up = shift(up, "first", 1)
    down = shift(down, "first", -1)
    rest = own_rest + got_rest.astype(F32)
    rest, up, down = tie((rest, up, down))
    none = jnp.zeros_like(up)
    low, high = tie(
        (
            (rest[:16] + jnp.concatenate([up, none]).astype(F32)).astype(BF16),
            (rest[16:32] + jnp.concatenate([down, none]).astype(F32)).astype(BF16),
        )
    )
    low = shift(low, "first", 1)
    high = shift(high, "first", -1)
    low, high = tie((low, high))
    here = rest[32:] + low.astype(F32) + jnp.concatenate([high[8:], high[:8]]).astype(F32)
    total = here.reshape(4, CAPO, BS, BS)
    out, *sent = tie((total[0], *(total[k].astype(BF16) for k in (2, 1, 3))))
    got = tie(tuple(shift(value, "second", k) for value, k in zip(sent, (2, 1, 3))))
    for value in got:
        out = out + value.astype(F32)
    return out


def on_device(
    features, out_grad, gate_pre, up_pre, hidden_grad, block_hidden, block_feature, block_slot
):
    tok_rows = features.shape[0]
    n_col = lax.axis_size("col")
    scale = 1.0 / math.sqrt(tok_rows * lax.axis_size("tok"))
    ring = [
        (t * n_col + z, t * n_col + (z + (1 if t % NC == 0 else -1)) % n_col)
        for t in range(NX * NY * NC)
        for z in range(n_col)
    ]
    table = tile_table(
        block_hidden, block_feature, block_slot, n_col, features.shape[1] // BS, gate_pre.shape[1] // BS
    )
    hid = hidden_blocks(gate_pre, up_pre, hidden_grad)
    tiles = tuple(
        jnp.zeros((size, BS, BS), BF16 if g < 2 else F32) for g, (base, size) in enumerate(GROUPS)
    )
    tie = lax.optimization_barrier
    chunks = [features, out_grad]
    made = 0
    for segment in range(2, 2 * n_col):
        value = chunks[segment - 2]
        if segment == 4:
            value, table, hid, tiles = tie((value, table, hid, tiles))
        if segment > 4:
            tiles = make_tiles(made, table, chunks[made], hid, tiles, scale)
            made += 1
            value, tiles = tie((value, tiles))
        chunks.append(lax.ppermute(value, ("tok", "col"), ring))
    for segment in range(made, 2 * n_col):
        tiles = make_tiles(segment, table, chunks[segment], hid, tiles, scale)
    return reduce_tiles(*tiles)[None]


def solution(mesh):
    in_specs = (P("tok", "col"),) * 5 + (P(), P(), P())
    return jax.shard_map(
        on_device,
        mesh=mesh,
        in_specs=in_specs,
        out_specs=P("col", "tok", None, None),
        check_vma=False,
    )
```

```python
import math

import jax
import jax.numpy as jnp
from jax import lax
from jax.experimental import pallas as pl
from jax.experimental.pallas import tpu as pltpu
from jax.sharding import PartitionSpec as P

BS = 128
NX, NY, NC = 4, 4, 2
CAPO = 4
UNROLL = 4
PLACES = NX * NY * NC * CAPO
GROUPS = ((0, 16), (16, 48), (64, 16), (80, 48))
F32, BF16 = jnp.float32, jnp.bfloat16
ANY = pl.BlockSpec(memory_space=pl.ANY)


def gate_kernel(gate_ref, up_ref, grad_ref, out_ref):
    for k in range(out_ref.shape[1]):
        at = (slice(None), pl.ds(k * BS, BS))
        gate = gate_ref[at].astype(F32)
        up = up_ref[at].astype(F32)
        grad = grad_ref[at].astype(F32)
        sig = jax.nn.sigmoid(gate)
        act = gate * sig
        out_ref[0, k] = (grad * up * sig * (1.0 + gate * (1.0 - sig))).astype(BF16)
        out_ref[1, k] = (grad * act).astype(BF16)
        out_ref[2, k] = (act * up).astype(BF16)


def hidden_blocks(gate_pre, up_pre, hidden_grad):
    rows, width = gate_pre.shape
    blocks = width // BS
    each = blocks // 2
    spec = pl.BlockSpec((rows, each * BS), lambda i: (0, i))
    out = pl.pallas_call(
        gate_kernel,
        grid=(blocks // each,),
        in_specs=[spec] * 3,
        out_specs=pl.BlockSpec((3, each, rows, BS), lambda i: (0, i, 0, 0)),
        out_shape=jax.ShapeDtypeStruct((3, blocks, rows, BS), BF16),
        cost_estimate=pl.CostEstimate(flops=0, bytes_accessed=12 * rows * width * 2, transcendentals=0),
        compiler_params=pltpu.CompilerParams(vmem_limit_bytes=16 * 2**20),
        name="gate_blocks",
    )(gate_pre, up_pre, hidden_grad)
    return out.reshape(3 * blocks, rows, BS)


def tile_kernel(segment, scale, tab_ref, chunk_ref, hid_ref, *refs):
    outs, (stage, stage16, sems) = refs[-7:-3], refs[-3:]
    unroll = 2 if segment % 2 else UNROLL
    begin, end = tab_ref[PLACES + segment], tab_ref[PLACES + segment + 1]
    rounds = (end - begin + unroll - 1) // unroll

    def tile(i):
        entry = tab_ref[jnp.minimum(i, end - 1)] // PLACES
        feat = chunk_ref[:, pl.ds(pl.multiple_of((entry // 64) % 8 * BS, BS), BS)]
        hid = hid_ref[entry % 64]
        left, right = (hid, feat) if segment % 2 else (feat, hid)
        out = lax.dot_general(left, right, (((0,), (0,)), ((), ())), preferred_element_type=F32)
        return out * scale

    def each_copy(n, k, act):
        i = begin + n * unroll + k
        at = (n % 2) * unroll + k
        p = tab_ref[jnp.minimum(i, end - 1)] % PLACES
        for g, (base, size) in enumerate(GROUPS):

            @pl.when((i < end) & (p >= base) & (p < base + size))
            def _():
                held = stage16 if outs[g].dtype == BF16 else stage
                act(pltpu.make_async_copy(held.at[at], outs[g].at[p - base], sems.at[at]))

    def start(copy):
        copy.start()

    def wait(copy):
        copy.wait()

    def body(n, carry):
        @pl.when(n >= 2)
        def _():
            for k in range(unroll):
                each_copy(n - 2, k, wait)

        made = [tile(begin + n * unroll + k) for k in range(unroll)]
        for k in range(unroll):
            stage[(n % 2) * unroll + k] = made[k]
            stage16[(n % 2) * unroll + k] = made[k].astype(BF16)
        for k in range(unroll):
            each_copy(n, k, start)
        return carry

    lax.fori_loop(0, rounds, body, 0)
    for back in (2, 1):

        @pl.when(rounds >= back)
        def _():
            for k in range(unroll):
                each_copy(rounds - back, k, wait)


def make_tiles(segment, table, chunk, hid, tiles, scale):
    def body(*refs):
        tile_kernel(segment, scale, *refs)

    return pl.pallas_call(
        body,
        in_specs=[
            pl.BlockSpec(memory_space=pltpu.SMEM),
            pl.BlockSpec(memory_space=pltpu.VMEM),
            pl.BlockSpec(memory_space=pltpu.VMEM),
            *[ANY] * len(tiles),
        ],
        out_specs=[ANY] * len(tiles),
        out_shape=[jax.ShapeDtypeStruct(t.shape, t.dtype) for t in tiles],
        scratch_shapes=[
            pltpu.VMEM((2 * UNROLL, BS, BS), F32),
            pltpu.VMEM((2 * UNROLL, BS, BS), BF16),
            pltpu.SemaphoreType.DMA((2 * UNROLL,)),
        ],
        input_output_aliases={3 + g: g for g in range(len(tiles))},
        cost_estimate=pl.CostEstimate(flops=0, bytes_accessed=4 * 2**20, transcendentals=0),
        compiler_params=pltpu.CompilerParams(vmem_limit_bytes=12 * 2**20),
        name=f"tiles_{segment}",
    )(table, chunk, hid, *tiles)


def place():
    me = lax.axis_index("tok")
    return me // (NY * NC), (me // NC) % NY, me % NC


def shift(value, kind, by):
    pairs = []
    for i in range(NX * NY * NC):
        x, y, c = i // (NY * NC), (i // NC) % NY, i % NC
        if kind == "core":
            c = 1 - c
        elif kind == "first":
            x, y = ((x + by) % NX, y) if c == 0 else (x, (y + by) % NY)
        else:
            x, y = (x, y ^ by) if c == 0 else (x ^ by, y)
        pairs.append((i, (x * NY + y) * NC + c))
    return lax.ppermute(value, "tok", pairs)


def slot_order():
    x, y, c = place()
    p = jnp.arange(PLACES, dtype=jnp.int32)
    b = (p // 8) % 8
    d1 = jnp.where(b < 2, 2, jnp.where(b < 4, 1, jnp.where(b < 6, 3, 0)))
    upper = (b == 1) | (b == 3) | (b == 4) | (b == 7)
    d2 = (p // CAPO) % 2 + 2 * upper.astype(jnp.int32)
    to_c = jnp.where(p < 64, 1 - c, c)
    to_x = jnp.where(to_c == 0, (x + d1) % NX, x ^ d2)
    to_y = jnp.where(to_c == 0, y ^ d2, (y + d1) % NY)
    return ((to_x * NY + to_y) * NC + to_c) * CAPO + p % CAPO


def tile_table(block_hidden, block_feature, block_slot, n_col, per, hid_per):
    col = lax.axis_index("col")
    matrix = jnp.arange(3, dtype=jnp.int32)[:, None]
    down = (matrix == 2).astype(jnp.int32)
    ahead = jnp.where(place()[2] == 0, 1, -1)
    step = (ahead * (col - block_feature // per)) % n_col
    hid = matrix * hid_per + block_hidden % hid_per
    value = 1 + (((step * 2 + down) * 8 + block_feature % per) * 64 + hid)
    value = jnp.where(block_hidden // hid_per == col, value, 0).reshape(-1)
    hit = slot_order()[:, None] == block_slot.reshape(-1)[None, :]
    code = jnp.sum(jnp.where(hit, value[None, :], 0), axis=1)
    p = jnp.arange(PLACES, dtype=jnp.int32)
    entry = jnp.where(code > 0, (code - 1) * PLACES + p, p)
    key = jnp.where(code > 0, (code - 1) // 512, 2 * n_col) * PLACES + p
    rank = jnp.sum((key[None, :] < key[:, None]).astype(jnp.int32), axis=1)
    ordered = jnp.sum(jnp.where(rank[None, :] == p[:, None], entry[None, :], 0), axis=1)
    bounds = jnp.arange(24, dtype=jnp.int32) * PLACES
    starts = jnp.sum((key[None, :] < bounds[:, None]).astype(jnp.int32), axis=1)
    return jnp.concatenate([ordered, starts])


def reduce_tiles(send_now, send_rest, own_now, own_rest):
    tie = lax.optimization_barrier
    got_now = shift(send_now, "core", 1)
    send_rest, got_now = tie((send_rest, got_now))
    got_rest = shift(send_rest, "core", 1)
    now = (own_now + got_now.astype(F32)).astype(BF16)
    up, down = tie((now[:8], now[8:]))
    up = shift(up, "first", 1)
    down = shift(down, "first", -1)
    rest = own_rest + got_rest.astype(F32)
    rest, up, down = tie((rest, up, down))
    none = jnp.zeros_like(up)
    low, high = tie(
        (
            (rest[:16] + jnp.concatenate([up, none]).astype(F32)).astype(BF16),
            (rest[16:32] + jnp.concatenate([down, none]).astype(F32)).astype(BF16),
        )
    )
    low = shift(low, "first", 1)
    high = shift(high, "first", -1)
    low, high = tie((low, high))
    here = rest[32:] + low.astype(F32) + jnp.concatenate([high[8:], high[:8]]).astype(F32)
    total = here.reshape(4, CAPO, BS, BS)
    out, *sent = tie((total[0], *(total[k].astype(BF16) for k in (2, 1, 3))))
    got = tie(tuple(shift(value, "second", k) for value, k in zip(sent, (2, 1, 3))))
    for value in got:
        out = out + value.astype(F32)
    return out


def on_device(
    features, out_grad, gate_pre, up_pre, hidden_grad, block_hidden, block_feature, block_slot
):
    tok_rows = features.shape[0]
    n_col = lax.axis_size("col")
    scale = 1.0 / math.sqrt(tok_rows * lax.axis_size("tok"))
    ring = [
        (t * n_col + z, t * n_col + (z + (1 if t % NC == 0 else -1)) % n_col)
        for t in range(NX * NY * NC)
        for z in range(n_col)
    ]
    table = tile_table(
        block_hidden, block_feature, block_slot, n_col, features.shape[1] // BS, gate_pre.shape[1] // BS
    )
    hid = hidden_blocks(gate_pre, up_pre, hidden_grad)
    tiles = tuple(
        jnp.zeros((size, BS, BS), BF16 if g < 2 else F32) for g, (base, size) in enumerate(GROUPS)
    )
    tie = lax.optimization_barrier
    chunks = [features, out_grad]
    made = 0
    for segment in range(2, 2 * n_col):
        value = chunks[segment - 2]
        if segment == 4:
            value, table, hid, tiles = tie((value, table, hid, tiles))
        if segment > 4:
            tiles = make_tiles(made, table, chunks[made], hid, tiles, scale)
            made += 1
            value, tiles = tie((value, tiles))
        chunks.append(lax.ppermute(value, ("tok", "col"), ring))
    for segment in range(made, 2 * n_col):
        tiles = make_tiles(segment, table, chunks[segment], hid, tiles, scale)
    return reduce_tiles(*tiles)[None]


def solution(mesh):
    in_specs = (P("tok", "col"),) * 5 + (P(), P(), P())
    return jax.shard_map(
        on_device,
        mesh=mesh,
        in_specs=in_specs,
        out_specs=P("col", "tok", None, None),
        check_vma=False,
    )
```
